128 devices in a mesh: grp: 4 (over x), seq: 32 (over z, y, core).
Axes of the slice: x: 4, y: 4, z: 4, core: 2. Of those that a mesh axis runs over, the one named last changes fastest.
Arguments:
- owned_patches: bfloat16 [4, 4096, 1152], P('grp', 'seq'), may hold values from -6 to 6
- send_rows: int32 [4, 32, 128], P('grp', 'seq'), may hold values from 0 to 127, each once within a row
- receive_slot: int32 [4, 32, 128], P('grp', 'seq'), may hold values from 0 to 127, each once within a row
- segment_ids: int32 [4, 4096], P('grp', 'seq'), may hold values from 0 to 15, never falling along the last dimension, each value on 1 to 2560 neighbouring positions
- class_label: int32 [4, 16], P('grp'), may hold values from 0 to 999
- drop_mask: int32 [4, 16], P('grp'), may hold values 0 or 1
- class_table: bfloat16 [1001, 1152], replicated, may hold values from -6 to 6
- modulation_weight: bfloat16 [1152, 3456], replicated, may hold values from -0.1875 to 0.1875
- attention_in: bfloat16 [1152, 1728], replicated, may hold values from -0.1875 to 0.1875
- attention_out: bfloat16 [576, 1152], replicated, may hold values from -0.25 to 0.25
- cotangent: bfloat16 [4, 4096, 1152], P('grp', 'seq'), may hold values from -6 to 6
Outputs:
- layer_output: bfloat16 [4, 4096, 1152], P('grp', 'seq')
- owner_gradient: bfloat16 [4, 4096, 1152], P('grp', 'seq')
- gradient_in: bfloat16 [1152, 1728], replicated
- gradient_out: bfloat16 [576, 1152], replicated
The draws below stay inside these ranges and needn't reach their ends.
Inputs may be any that keep to these rules, and one draw needn't show every extreme that they name: `send_rows`: for owner shard s of a group, entries 4 * d to 4 * d + 3 name, in slot order, the local rows that go to packed shard d; every local row once. `receive_slot`: packed row r of packed shard d takes slot c of what owner shard s sends to d, where the entry is 4 * s + c; every slot once. `segment_ids`: never falling along a group's tokens; every image has 1 to 2560 tokens, one exactly 2560.
All inputs are finite; a program needn't handle non-finite values. No bound on the sum of `drop_mask` on one device may be relied on, other than what follows from the above.
Results may differ from the reference program's by a relative error of at most 0.015.
Values may be sent and summed in bfloat16 or wider, within the bound.
No kernel may reach another device: no remote copies, remote signals or barrier semaphores. Data moves between devices by JAX's collectives and lax.ppermute only.
A program may use at most 128 MiB of HBM per device.

```python
import math
import jax
import jax.numpy as jnp
import numpy as np
from jax import lax

D = 1152
HEADS = 8
HEAD = 72
ATT = 576
CLASSES = 1000
TOK_DEV = 128
IMAGES = 16
SEQ_TOK = 4096
MOST = 2560
ALL_TOK = 16384
N_GRP = 4
N_SEQ = 32


def plant(array, own_key, smallest, top_value):
    index_at = [jax.random.randint(jax.random.fold_in(own_key, axis), (), 0, length) for axis, length in enumerate(array.shape)]
    widest = array.shape.index(max(array.shape))
    neighbour = index_at[:widest] + [(index_at[widest] + 1) % array.shape[widest]] + index_at[widest + 1:]
    return array.at[tuple(index_at)].set(smallest).at[tuple(neighbour)].set(top_value)


def level_of(rng, dims, split, low, top_value):
    def one(dim, shards_of):
        heights = jax.random.uniform(jax.random.fold_in(jax.random.fold_in(rng, 6), dim), (shards_of,), jnp.float32, low / len(split), top_value / len(split))
        return jnp.repeat(jnp.exp(heights), dims[dim] // shards_of).reshape((-1,) + (1,) * (len(dims) - dim - 1))

    level = one(*split[0])
    for cut in split[1:]:
        level = level * one(*cut)
    return level


def split_up(count, total, most, skew):
    portions = [(1 << 20) // math.isqrt(rank ** skew) + 1 for rank in range(2, count + 1)]
    surplus, counts = total - most - (count - 1), [1] * (count - 1)
    while surplus > 0:
        movable = [i for i in range(count - 1) if counts[i] < most]
        pool, left = sum([portions[i] for i in movable]), surplus
        for i in movable:
            extra = min(most - counts[i], max(1, left * portions[i] // pool), surplus)
            counts[i] = counts[i] + extra
            surplus = surplus - extra
    return np.array([most] + counts)


def uneven_parts(stream_key, amount, total, reach, lean):
    if amount == 2:
        one = jax.random.randint(stream_key, (), max(1, total - reach), min(reach, total - 1) + 1)
        return jnp.stack([one, total - one])
    tallies = jnp.asarray(split_up(amount, total, reach, lean), jnp.int32)
    pairs = (amount - 1) // 2
    source_of, receiver = tallies[1:1 + 2 * pairs:2], tallies[2:2 + 2 * pairs:2]
    room = jnp.minimum(source_of - 1, reach - receiver)
    passed = jax.random.randint(jax.random.fold_in(stream_key, 1), (pairs,), 0, 1 << 20) % (room + 1)
    tallies = tallies.at[1:1 + 2 * pairs:2].set(source_of - passed).at[2:2 + 2 * pairs:2].set(receiver + passed)
    return tallies[jax.random.permutation(jax.random.fold_in(stream_key, 2), amount)]


def bell_draw(stream_key, dims, deviation, reach, cuts=(), dtype=jnp.bfloat16):
    factor_of = level_of(stream_key, dims, cuts, -0.22, 0.18) if cuts else 1.0
    drawn = jax.random.normal(stream_key, dims, jnp.float32) * deviation * factor_of
    return jnp.minimum(jnp.maximum(drawn, -reach), reach).astype(dtype)


def setup_inputs(seed: int = 0) -> dict:
    key_list = jax.random.split(jax.random.key(seed), 12)
    owned_patches = bell_draw(key_list[0], (N_GRP, SEQ_TOK, D), 1.0, 6.0, ((0, 4), (1, 32)))
    send_rows = jax.vmap(lambda own: jax.random.permutation(own, TOK_DEV))(jax.random.split(key_list[1], N_GRP * N_SEQ)).reshape((N_GRP, N_SEQ, TOK_DEV)).astype(jnp.int32)
    receive_slot = jax.vmap(lambda own: jax.random.permutation(own, TOK_DEV))(jax.random.split(key_list[2], N_GRP * N_SEQ)).reshape((N_GRP, N_SEQ, TOK_DEV)).astype(jnp.int32)
    segment_ids = jax.vmap(lambda own: jnp.searchsorted(jnp.cumsum(uneven_parts(own, IMAGES, SEQ_TOK, MOST, 2)), jnp.arange(SEQ_TOK), side="right"))(jax.random.split(key_list[3], N_GRP)).reshape((N_GRP, SEQ_TOK)).astype(jnp.int32)
    class_label = plant(jax.random.randint(key_list[4], (N_GRP, IMAGES), 0, CLASSES), jax.random.fold_in(key_list[4], 1), 0, CLASSES - 1).astype(jnp.int32)
    drop_mask = plant((jax.random.randint(key_list[5], (N_GRP, IMAGES), 0, 10) < 1).astype(jnp.int32), jax.random.fold_in(key_list[5], 1), 0, 1)
    class_table = bell_draw(key_list[6], (CLASSES + 1, D), 1.0, 6.0)
    modulation_weight = bell_draw(key_list[7], (D, 3 * D), D ** -0.5, 0.1875)
    attention_in = bell_draw(key_list[8], (D, 3 * ATT), D ** -0.5, 0.1875)
    attention_out = bell_draw(key_list[9], (ATT, D), ATT ** -0.5, 0.25)
    cotangent = bell_draw(key_list[10], (N_GRP, SEQ_TOK, D), 1.0, 6.0, ((0, 4), (1, 32)))
    return dict(owned_patches=owned_patches, send_rows=send_rows, receive_slot=receive_slot, segment_ids=segment_ids, class_label=class_label, drop_mask=drop_mask, class_table=class_table, modulation_weight=modulation_weight, attention_in=attention_in, attention_out=attention_out, cotangent=cotangent)


EPSILON = 1e-06

def normalize(values):
    center = values - lax.optimization_barrier(jnp.mean(values, axis=-1, keepdims=True))
    spread = lax.optimization_barrier(jnp.mean(center * center, axis=-1, keepdims=True))
    inverse_spread = lax.rsqrt(spread + EPSILON)
    return (center * inverse_spread, inverse_spread)

def rounded(values):
    return lax.optimization_barrier(values.astype(jnp.bfloat16)).astype(jnp.float32)

def take_rows(table, positions):
    return jnp.take(table, positions, axis=0)

def place_rows(source, positions):
    return jnp.zeros_like(source).at[positions].set(source)

def to_packed(owned, send_rows, receive_slot):
    shards, per_shard = send_rows.shape
    slot_count = per_shard // shards
    feature_width = owned.shape[-1]
    by_owner = owned.reshape(shards, per_shard, feature_width)
    outgoing = jax.vmap(take_rows)(by_owner, send_rows)
    incoming = outgoing.reshape(shards, shards, slot_count, feature_width).transpose(1, 0, 2, 3)
    incoming = incoming.reshape(shards, per_shard, feature_width)
    return jax.vmap(take_rows)(incoming, receive_slot).reshape(shards * per_shard, feature_width)

def to_owners(packed_rows, send_rows, receive_slot):
    shards, per_shard = send_rows.shape
    slot_count = per_shard // shards
    feature_width = packed_rows.shape[-1]
    by_packed = packed_rows.reshape(shards, per_shard, feature_width)
    slotted = jax.vmap(place_rows)(by_packed, receive_slot)
    returned = slotted.reshape(shards, shards, slot_count, feature_width).transpose(1, 0, 2, 3)
    returned = returned.reshape(shards, per_shard, feature_width)
    return jax.vmap(place_rows)(returned, send_rows).reshape(shards * per_shard, feature_width)

def exponent(query_block, key_heads, image_query, image_keys):
    logits = jnp.einsum('qhe,khe->qhk', query_block, key_heads) * HEAD ** (-0.5)
    joined = (image_query[:, None] == image_keys[None, :])[:, None, :]
    return jnp.exp(jnp.where(joined, logits, -jnp.inf))

def group_forward(query_heads, key_heads, value_heads, images):
    total_rows = query_heads.shape[0]
    block_rows = math.gcd(total_rows, 512)
    block_count = total_rows // block_rows

    def one_block(pair):
        query_block, image_block = pair
        powers = exponent(query_block, key_heads, image_block, images)
        totals = lax.optimization_barrier(jnp.sum(powers, axis=-1))
        weighted = jnp.einsum('qhk,khe->qhe', rounded(powers), value_heads)
        return (weighted, totals)
    weighted, totals = lax.map(one_block, (query_heads.reshape(block_count, block_rows, HEADS, HEAD), images.reshape(block_count, block_rows)))
    return (weighted.reshape(total_rows, HEADS, HEAD), totals.reshape(total_rows, HEADS))

def group_backward(query_heads, key_heads, value_heads, cotangent_heads, images, totals, delta_rows):
    total_rows = query_heads.shape[0]
    block_rows = math.gcd(total_rows, 512)
    block_count = total_rows // block_rows

    def one_block(carried, pieces):
        query_block, cotangent_block, image_block, total_block, delta_block = pieces
        weights = exponent(query_block, key_heads, image_block, images) / total_block[:, :, None]
        weight_cotangent = jnp.einsum('qhe,khe->qhk', cotangent_block, value_heads)
        score_cotangent = rounded(weights * (weight_cotangent - delta_block[:, :, None]))
        query_part = jnp.einsum('qhk,khe->qhe', score_cotangent, key_heads)
        key_sum = carried[0] + jnp.einsum('qhk,qhe->khe', score_cotangent, query_block)
        value_sum = carried[1] + jnp.einsum('qhk,qhe->khe', rounded(weights), cotangent_block)
        return ((key_sum, value_sum), query_part)
    zeros_start = jnp.zeros(key_heads.shape, jnp.float32)
    pieces = (query_heads.reshape(block_count, block_rows, HEADS, HEAD), cotangent_heads.reshape(block_count, block_rows, HEADS, HEAD), images.reshape(block_count, block_rows), totals.reshape(block_count, block_rows, HEADS), delta_rows.reshape(block_count, block_rows, HEADS))
    (key_sum, value_sum), query_parts = lax.scan(one_block, (zeros_start, zeros_start), pieces)
    return (query_parts.reshape(total_rows, HEADS, HEAD), key_sum, value_sum)

def reference(owned_patches, send_rows, receive_slot, segment_ids, class_label, drop_mask, class_table, modulation_weight, attention_in, attention_out, cotangent):
    factor = HEAD ** (-0.5)
    outputs = []
    owner_rows = []
    in_total = jnp.zeros(attention_in.shape, jnp.float32)
    out_total = jnp.zeros(attention_out.shape, jnp.float32)
    for group in range(owned_patches.shape[0]):
        images = segment_ids[group]
        packed = to_packed(owned_patches[group], send_rows[group], receive_slot[group])
        chosen = jnp.where(drop_mask[group] == 1, CLASSES, class_label[group]).astype(jnp.int32)
        condition = jnp.take(class_table, chosen, axis=0)
        activated = jax.nn.silu(condition.astype(jnp.float32)).astype(jnp.bfloat16)
        modulation = jnp.dot(activated, modulation_weight, preferred_element_type=jnp.float32)
        per_token = jnp.take(modulation, images, axis=0)
        shift_rows = per_token[:, :D]
        scale_rows = per_token[:, D:2 * D]
        gate_rows = per_token[:, 2 * D:]
        row_values = packed.astype(jnp.float32)
        normed, inverse_spread = normalize(row_values)
        hidden = (normed * (1.0 + scale_rows) + shift_rows).astype(jnp.bfloat16)
        projected_f = jnp.dot(hidden, attention_in, preferred_element_type=jnp.float32)
        heads_all = rounded(projected_f).reshape(SEQ_TOK, 3, HEADS, HEAD)
        query_heads = heads_all[:, 0]
        key_heads = heads_all[:, 1]
        value_heads = heads_all[:, 2]
        weighted, totals = group_forward(query_heads, key_heads, value_heads, images)
        attended_f = (weighted / totals[:, :, None]).reshape(SEQ_TOK, ATT)
        attended = attended_f.astype(jnp.bfloat16)
        attended_heads = rounded(attended_f).reshape(SEQ_TOK, HEADS, HEAD)
        projected = jnp.dot(attended, attention_out, preferred_element_type=jnp.float32)
        outputs.append((row_values + gate_rows * projected).astype(jnp.bfloat16))
        upstream = cotangent[group].astype(jnp.float32)
        branch = (gate_rows * upstream).astype(jnp.bfloat16)
        out_total = out_total + jnp.dot(attended.T, branch, preferred_element_type=jnp.float32)
        attended_cot_f = jnp.dot(branch, attention_out.T, preferred_element_type=jnp.float32)
        cotangent_heads = rounded(attended_cot_f).reshape(SEQ_TOK, HEADS, HEAD)
        delta_rows = lax.optimization_barrier(jnp.sum(cotangent_heads * attended_heads, axis=-1))
        query_sum, key_sum, value_sum = group_backward(query_heads, key_heads, value_heads, cotangent_heads, images, totals, delta_rows)
        input_cotangent = jnp.concatenate([(query_sum * factor).reshape(SEQ_TOK, ATT).astype(jnp.bfloat16), (key_sum * factor).reshape(SEQ_TOK, ATT).astype(jnp.bfloat16), value_sum.reshape(SEQ_TOK, ATT).astype(jnp.bfloat16)], axis=1)
        in_total = in_total + jnp.dot(hidden.T, input_cotangent, preferred_element_type=jnp.float32)
        hidden_cotangent = jnp.dot(input_cotangent, attention_in.T, preferred_element_type=jnp.float32)
        scaled_cot = hidden_cotangent * (1.0 + scale_rows)
        packed_cotangent = upstream + inverse_spread * (scaled_cot - lax.optimization_barrier(jnp.mean(scaled_cot, axis=-1, keepdims=True)) - normed * lax.optimization_barrier(jnp.mean(scaled_cot * normed, axis=-1, keepdims=True)))
        owner_rows.append(to_owners(packed_cotangent.astype(jnp.bfloat16), send_rows[group], receive_slot[group]))
    norm_factor = ALL_TOK ** (-0.5)
    return (jnp.stack(outputs), jnp.stack(owner_rows), (in_total * norm_factor).astype(jnp.bfloat16), (out_total * norm_factor).astype(jnp.bfloat16))
```

```python
import math

import jax
import jax.numpy as jnp
from jax import lax
from jax.experimental import pallas as pl
from jax.experimental.pallas import tpu as pltpu
from jax.sharding import PartitionSpec as P

HEADS = 8
CLASSES = 1000
EPSILON = 1e-06

D = 1152
ATT = 576
HEAD = 72
ROWS = 80
TOK = 128
SETS = 4
PEERS = 8
OWN = PEERS * TOK
KEYS = SETS * OWN
QUERY_TILE = 256
KEY_TILE = 512
FAR = -1e30

F32 = jnp.float32
BF16 = jnp.bfloat16
FACTOR = HEAD ** (-0.5)
TO_BASE2 = FACTOR * math.log2(math.e)

HEAD_GROUPS = [[r + SETS * h for h in range(PEERS)] for r in range(SETS)]
SWAP_CORE = [(i, i ^ 1) for i in range(32)]
SWAP_CHIP = [(i, i ^ 2) for i in range(32)]

LEFT = (((0,), (0,)), ((), ()))
LAST = (((1,), (1,)), ((), ()))


def dot(a, b):
    return jnp.dot(a, b, preferred_element_type=F32)


def call(kernel, outs, scratch=(), flops=0, smem=0, n_in=1, limit=48):
    vmem = pl.BlockSpec(memory_space=pltpu.VMEM)
    scalar = pl.BlockSpec(memory_space=pltpu.SMEM)
    return pl.pallas_call(
        kernel,
        out_shape=outs,
        in_specs=[scalar] * smem + [vmem] * (n_in - smem),
        out_specs=[vmem] * len(outs),
        scratch_shapes=list(scratch),
        compiler_params=pltpu.CompilerParams(vmem_limit_bytes=limit * 1024 * 1024),
        cost_estimate=pl.CostEstimate(flops=flops, bytes_accessed=4_000_000, transcendentals=0),
    )


def shape(*dims):
    return jax.ShapeDtypeStruct(dims, BF16)


def image_rows(seg, table):
    spots = lax.broadcasted_iota(jnp.int32, (16, TOK), 0)
    one_hot = (spots == seg).astype(F32)
    return lax.dot_general(
        one_hot, table, LEFT, precision=lax.Precision.HIGHEST, preferred_element_type=F32
    )


def permutation(positions):
    spots = lax.broadcasted_iota(jnp.int32, (TOK, TOK), 0)
    return (spots == positions).astype(F32).astype(BF16)


def normalize(values):
    center = values - jnp.mean(values, axis=-1, keepdims=True)
    spread = jnp.mean(center * center, axis=-1, keepdims=True)
    inverse_spread = lax.rsqrt(spread + EPSILON)
    return (center * inverse_spread, inverse_spread)


def branch_kernel(seg_ref, gate_ref, cot_ref, wo_ref, branch_ref, back_ref):
    gate = image_rows(seg_ref[...], gate_ref[...])
    branch = (gate * cot_ref[...].astype(F32)).astype(BF16)
    branch_ref[...] = branch
    turned = lax.dot_general(branch, wo_ref[...], LAST, preferred_element_type=F32).T
    pad = jnp.zeros((ROWS - HEAD, TOK), F32)
    for h in range(HEADS):
        block = jnp.concatenate([turned[h * HEAD : (h + 1) * HEAD], pad], axis=0)
        back_ref[h] = block.astype(BF16)


def enter_kernel(slot_ref, seg_ref, inc_ref, mod_ref, win_ref, back_ref, packed_ref, hidden_ref, out_ref):
    seg = seg_ref[...]
    packed = lax.dot_general(
        permutation(slot_ref[...]), inc_ref[...], LEFT, preferred_element_type=F32
    )
    packed_ref[...] = packed.astype(BF16)
    per_token = image_rows(seg, mod_ref[...])
    normed, _ = normalize(packed)
    hidden = (normed * (1.0 + per_token[:, D:]) + per_token[:, :D]).astype(BF16)
    hidden_ref[...] = hidden
    turned = dot(hidden, win_ref[...]).T
    spots = lax.broadcasted_iota(jnp.int32, (ROWS - HEAD, TOK), 0)
    zeros = jnp.zeros((ROWS - HEAD, TOK), F32)
    ids = jnp.where(spots == 0, seg.astype(F32), 0.0)
    ones = jnp.where(spots == 0, 1.0, jnp.where(spots <= 2, 1.0, 0.0))
    for h in range(HEADS):
        for part, (place, pad) in enumerate(((0, zeros), (2, ids), (3, ones))):
            first = part * ATT + h * HEAD
            block = jnp.concatenate([turned[first : first + HEAD], pad], axis=0)
            out_ref[h, place * ROWS : (place + 1) * ROWS] = block.astype(BF16)
        out_ref[h, ROWS : 2 * ROWS] = back_ref[h]


def attend_kernel(x_ref, a_ref, b_ref, c_ref, own_ref, keep_ref, send_ref, k_s, v_s, kt_s, vt_s, q_s, d_s, p_s, dk_s, dv_s):
    spots = lax.broadcasted_iota(jnp.int32, (16, TOK), 0).astype(F32)
    for j, (ref, base) in enumerate(((x_ref, 2 * ROWS), (a_ref, 0), (b_ref, 0), (c_ref, 0))):
        for s in range(PEERS):
            spot = pl.ds((j * PEERS + s) * TOK, TOK)
            keys = ref[s, base : base + ROWS]
            values = ref[s, base + ROWS : base + 2 * ROWS]
            kt_s[:, spot] = keys
            vt_s[:, spot] = values
            ids = keys.astype(F32)[HEAD : HEAD + 1]
            same = spots == ids
            wide = jnp.concatenate(
                [keys.astype(F32), same.astype(F32), jnp.zeros((TOK - ROWS - 16, TOK), F32)], axis=0
            )
            k_s[spot, :] = wide.T.astype(BF16)
            wide = jnp.concatenate(
                [values.astype(F32), jnp.zeros((TOK - ROWS, TOK), F32)], axis=0
            )
            v_s[spot, :] = wide.T.astype(BF16)
            if j == 0:
                q_s[0:ROWS, spot] = ref[s, 0:ROWS]
                q_s[ROWS : ROWS + 16, spot] = jnp.where(same, 0.0, FAR).astype(BF16)
                q_s[ROWS + 16 :, spot] = jnp.zeros((TOK - ROWS - 16, TOK), BF16)
                d_s[:, spot] = ref[s, ROWS : 2 * ROWS]
    dk_s[...] = jnp.zeros_like(dk_s)
    dv_s[...] = jnp.zeros_like(dv_s)

    def query_tile(block, carry):
        columns = pl.ds(pl.multiple_of(block * QUERY_TILE, QUERY_TILE), QUERY_TILE)
        queries = q_s[:, columns]

        def forward(tile, total):
            rows = pl.ds(pl.multiple_of(tile * KEY_TILE, KEY_TILE), KEY_TILE)
            powers = jnp.exp2(dot(k_s[rows, :], queries) * TO_BASE2).astype(BF16)
            p_s[rows, :] = powers
            return total + dot(vt_s[:, rows], powers)

        summed = lax.fori_loop(
            0, KEYS // KEY_TILE, forward, jnp.zeros((ROWS, QUERY_TILE), F32), unroll=2
        )
        totals = summed[HEAD : HEAD + 1]
        inverse = 1.0 / totals
        attended = (summed[0:HEAD] / totals).astype(BF16).astype(F32)
        cot = d_s[:, columns]
        cot_wide = cot.astype(F32)
        delta = -jnp.sum(cot_wide[0:HEAD] * attended, axis=0, keepdims=True)
        high = delta.astype(BF16).astype(F32)
        middle = (delta - high).astype(BF16).astype(F32)
        low = delta - high - middle
        lines = lax.broadcasted_iota(jnp.int32, (ROWS - HEAD, QUERY_TILE), 0)
        pad = jnp.where(lines == 0, high, jnp.where(lines == 1, middle, jnp.where(lines == 2, low, 0.0)))
        shifted = jnp.concatenate(
            [cot_wide[0:HEAD], pad, jnp.zeros((TOK - ROWS, QUERY_TILE), F32)], axis=0
        ).astype(BF16)

        def backward(tile, total):
            rows = pl.ds(pl.multiple_of(tile * KEY_TILE, KEY_TILE), KEY_TILE)
            weights = p_s[rows, :].astype(F32) * inverse
            score = (weights * dot(v_s[rows, :], shifted)).astype(BF16)
            dk_s[:, rows] += lax.dot_general(
                queries[0:ROWS], score, LAST, preferred_element_type=F32
            )
            dv_s[:, rows] += lax.dot_general(
                cot, weights.astype(BF16), LAST, preferred_element_type=F32
            )
            return total + dot(kt_s[:, rows], score)

        dq = lax.fori_loop(
            0, KEYS // KEY_TILE, backward, jnp.zeros((ROWS, QUERY_TILE), F32), unroll=2
        )
        attended = jnp.concatenate([attended, jnp.zeros((ROWS - HEAD, QUERY_TILE), F32)], axis=0)
        dq = dq * FACTOR
        for part in range(QUERY_TILE // TOK):
            lanes = slice(part * TOK, (part + 1) * TOK)
            own_ref[block * (QUERY_TILE // TOK) + part, 0:ROWS] = attended[:, lanes].astype(BF16)
            own_ref[block * (QUERY_TILE // TOK) + part, ROWS : 2 * ROWS] = dq[:, lanes].astype(BF16)
        return carry

    lax.fori_loop(0, OWN // QUERY_TILE, query_tile, 0)
    for j in range(SETS):
        ref = send_ref if j % 2 else keep_ref
        for s in range(PEERS):
            spot = pl.ds((j * PEERS + s) * TOK, TOK)
            ref[j // 2, s, 0:ROWS] = (dk_s[:, spot] * FACTOR).astype(BF16)
            ref[j // 2, s, ROWS : 2 * ROWS] = dv_s[:, spot].astype(BF16)


def weights_kernel(r_ref, own_ref, kept_ref, came_ref, hidden_ref, branch_ref, ret_ref, keep_ref, send_ref):
    position = r_ref[0]
    for s in range(PEERS):
        ret_ref[s, 0 : 2 * ROWS] = own_ref[s]
        both = kept_ref[s].astype(F32) + came_ref[s].astype(F32)
        ret_ref[s, 2 * ROWS :] = both.astype(BF16)

    def lined(place):
        return jnp.concatenate(
            [ret_ref[s, place * ROWS : (place + 1) * ROWS] for s in range(PEERS)], axis=1
        )

    inner = dot(jnp.concatenate([lined(1), lined(2), lined(3)], axis=0), hidden_ref[...])
    outer = dot(lined(0), branch_ref[...])
    for part in range(SETS):
        block = outer if part == 3 else inner[part * ROWS : (part + 1) * ROWS]
        block = block.astype(BF16)
        relative = position ^ part

        @pl.when((relative & 1) == 0)
        def _():
            keep_ref[relative >> 1] = block

        @pl.when((relative & 1) == 1)
        def _():
            send_ref[relative >> 1] = block


def leave_kernel(slot_ref, seg_ref, ret_ref, packed_ref, mod_ref, cot_ref, win_ref, wo_ref, out_ref, back_ref):
    def turned(place):
        return [
            ret_ref[h, place * ROWS : (place + 1) * ROWS].astype(F32)[0:HEAD] for h in range(HEADS)
        ]

    per_token = image_rows(seg_ref[...], mod_ref[...])
    scale = 1.0 + per_token[:, D : 2 * D]
    values = packed_ref[...].astype(F32)
    normed, inverse_spread = normalize(values)
    attended = jnp.concatenate(turned(0), axis=0).T.astype(BF16)
    out_ref[...] = (values + per_token[:, 2 * D :] * dot(attended, wo_ref[...])).astype(BF16)
    cot = jnp.concatenate(turned(1) + turned(2) + turned(3), axis=0).T.astype(BF16)
    scaled = lax.dot_general(cot, win_ref[...], LAST, preferred_element_type=F32) * scale
    packed_cot = cot_ref[...].astype(F32) + inverse_spread * (
        scaled
        - jnp.mean(scaled, axis=-1, keepdims=True)
        - normed * jnp.mean(scaled * normed, axis=-1, keepdims=True)
    )
    back_ref[...] = dot(permutation(slot_ref[...]), packed_cot.astype(BF16)).astype(BF16)


def shards(
    owned_patches,
    send_rows,
    receive_slot,
    segment_ids,
    class_label,
    drop_mask,
    class_table,
    modulation_weight,
    attention_in,
    attention_out,
    cotangent,
):
    slot, seg, cot = receive_slot[0], segment_ids, cotangent[0]
    spots = jnp.arange(TOK, dtype=jnp.int32)
    send_hot = send_rows[0, 0][:, None] == spots[None, :]
    outgoing = dot(send_hot.astype(BF16), owned_patches[0]).astype(BF16)
    incoming = lax.all_to_all(
        outgoing.reshape(32, TOK // 32, D), "seq", split_axis=0, concat_axis=0, tiled=True
    ).reshape(TOK, D)

    chosen = jnp.where(drop_mask[0] == 1, CLASSES, class_label[0])
    condition = jnp.take(class_table, chosen, axis=0)
    activated = jax.nn.silu(condition.astype(F32)).astype(BF16)
    modulation = dot(activated, modulation_weight)

    branch, back_heads = call(
        branch_kernel, (shape(TOK, D), shape(HEADS, ROWS, TOK)), n_in=4, flops=2 * TOK * D * ATT
    )(seg, modulation[:, 2 * D :], cot, attention_out)
    all_branch = lax.all_gather(branch, "seq", axis_index_groups=HEAD_GROUPS, tiled=True)
    packed, hidden, sending = call(
        enter_kernel,
        (shape(TOK, D), shape(TOK, D), shape(HEADS, 4 * ROWS, TOK)),
        n_in=6,
        flops=2 * TOK * D * 3 * ATT,
    )(slot, seg, incoming, modulation[:, : 2 * D], attention_in, back_heads)
    all_hidden = lax.all_gather(hidden, "seq", axis_index_groups=HEAD_GROUPS, tiled=True)
    mine = lax.all_to_all(
        sending, "seq", split_axis=0, concat_axis=0, axis_index_groups=HEAD_GROUPS, tiled=True
    )
    pairs = mine[:, 2 * ROWS :]
    from_chip = lax.ppermute(pairs, "seq", SWAP_CHIP)
    from_core = lax.ppermute(pairs, "seq", SWAP_CORE)
    from_both = lax.ppermute(from_chip, "seq", SWAP_CORE)

    own, keep, send = call(
        attend_kernel,
        (
            shape(PEERS, 2 * ROWS, TOK),
            shape(2, PEERS, 2 * ROWS, TOK),
            shape(2, PEERS, 2 * ROWS, TOK),
        ),
        n_in=4,
        flops=2 * 6 * OWN * KEYS * HEAD,
        scratch=(
            pltpu.VMEM((KEYS, TOK), BF16),
            pltpu.VMEM((KEYS, TOK), BF16),
            pltpu.VMEM((ROWS, KEYS), BF16),
            pltpu.VMEM((ROWS, KEYS), BF16),
            pltpu.VMEM((TOK, OWN), BF16),
            pltpu.VMEM((ROWS, OWN), BF16),
            pltpu.VMEM((KEYS, QUERY_TILE), BF16),
            pltpu.VMEM((ROWS, KEYS), F32),
            pltpu.VMEM((ROWS, KEYS), F32),
        ),
    )(mine, from_core, from_chip, from_both)

    def add(a, b):
        return (a.astype(F32) + b.astype(F32)).astype(BF16)

    came = lax.ppermute(send, "seq", SWAP_CORE)
    halves = add(keep, came)
    came = lax.ppermute(halves[1], "seq", SWAP_CHIP)
    position = (lax.axis_index("seq") & 3).astype(jnp.int32).reshape(1)
    returning, keep, send = call(
        weights_kernel,
        (shape(PEERS, 4 * ROWS, TOK), shape(2, ROWS, D), shape(2, ROWS, D)),
        smem=1,
        n_in=6,
        flops=2 * 4 * ROWS * OWN * D,
    )(position, own, halves[0], came, all_hidden, all_branch)

    came = lax.ppermute(send, "seq", SWAP_CORE)
    halves = add(keep, came)[:, :HEAD]
    came = lax.ppermute(halves[1], "seq", SWAP_CHIP)
    piece = add(halves[0], came)
    others = [
        lax.ppermute(piece, "grp", [(i, (i + k) % 4) for i in range(4)]) for k in (1, 3, 2)
    ]
    norm_factor = (4 * 32 * TOK) ** (-0.5)
    summed = piece.astype(F32)
    for other in others:
        summed = summed + other.astype(F32)
    summed = (summed * norm_factor).astype(BF16)
    summed, returning = lax.optimization_barrier((summed, returning))
    gathered = lax.all_gather(summed, "seq", tiled=True).reshape(HEADS, 4, HEAD, D)
    gradient_out = gathered[:, 3].reshape(ATT, D)
    gradient_in = gathered[:, :3].transpose(3, 1, 0, 2).reshape(D, 3 * ATT)

    returned = lax.all_to_all(
        returning, "seq", split_axis=0, concat_axis=0, axis_index_groups=HEAD_GROUPS, tiled=True
    )
    layer_output, back_order = call(
        leave_kernel,
        (shape(TOK, D), shape(TOK, D)),
        n_in=8,
        flops=2 * TOK * D * 4 * ATT,
    )(slot, seg, returned, packed, modulation, cot, attention_in, attention_out)
    home = lax.all_to_all(
        back_order.reshape(32, TOK // 32, D), "seq", split_axis=0, concat_axis=0, tiled=True
    ).reshape(TOK, D)
    home_hot = spots[:, None] == send_rows[0, 0][None, :]
    owner_gradient = dot(home_hot.astype(BF16), home).astype(BF16)
    return (layer_output[None], owner_gradient[None], gradient_in, gradient_out)


def solution(mesh):
    return jax.shard_map(
        shards,
        mesh=mesh,
        in_specs=(
            P("grp", "seq", None),
            P("grp", "seq", None),
            P("grp", "seq", None),
            P("grp", "seq"),
            P("grp", None),
            P("grp", None),
            P(),
            P(),
            P(),
            P(),
            P("grp", "seq", None),
        ),
        out_specs=(P("grp", "seq", None), P("grp", "seq", None), P(), P()),
        check_vma=False,
    )
```

```python
import math

import jax
import jax.numpy as jnp
from jax import lax
from jax.experimental import pallas as pl
from jax.experimental.pallas import tpu as pltpu
from jax.sharding import PartitionSpec as P

HEADS = 8
CLASSES = 1000
EPSILON = 1e-06

D = 1152
ATT = 576
HEAD = 72
ROWS = 80
TOK = 128
SETS = 4
PEERS = 8
OWN = PEERS * TOK
KEYS = SETS * OWN
QUERY_TILE = 1024
KEY_TILE = 512
FAR = -1e30

F32 = jnp.float32
BF16 = jnp.bfloat16
FACTOR = HEAD ** (-0.5)
TO_BASE2 = FACTOR * math.log2(math.e)

HEAD_GROUPS = [[PEERS * r + h for h in range(PEERS)] for r in range(SETS)]
UP = [(i, (i + PEERS) % 32) for i in range(32)]
DOWN = [(i, (i - PEERS) % 32) for i in range(32)]
ACROSS = [(i, (i + 2 * PEERS) % 32) for i in range(32)]
FRONT = PEERS // 2

LEFT = (((0,), (0,)), ((), ()))
LAST = (((1,), (1,)), ((), ()))


def dot(a, b):
    return jnp.dot(a, b, preferred_element_type=F32)


def call(kernel, outs, scratch=(), flops=0, smem=0, n_in=1, limit=20, far_in=(), far_out=()):
    vmem = pl.BlockSpec(memory_space=pltpu.VMEM)
    scalar = pl.BlockSpec(memory_space=pltpu.SMEM)
    hbm = pl.BlockSpec(memory_space=pltpu.MemorySpace.HBM)
    return pl.pallas_call(
        kernel,
        out_shape=outs,
        in_specs=[scalar] * smem + [hbm if i in far_in else vmem for i in range(smem, n_in)],
        out_specs=[hbm if i in far_out else vmem for i in range(len(outs))],
        scratch_shapes=list(scratch),
        compiler_params=pltpu.CompilerParams(vmem_limit_bytes=limit * 1024 * 1024),
        cost_estimate=pl.CostEstimate(flops=flops, bytes_accessed=4_000_000, transcendentals=0),
    )


def shape(*dims):
    return jax.ShapeDtypeStruct(dims, BF16)


def image_rows(seg, table):
    spots = lax.broadcasted_iota(jnp.int32, (16, TOK), 0)
    one_hot = (spots == seg).astype(F32)
    return lax.dot_general(
        one_hot, table, LEFT, precision=lax.Precision.HIGHEST, preferred_element_type=F32
    )


def permutation(positions):
    spots = lax.broadcasted_iota(jnp.int32, (TOK, TOK), 0)
    return (spots == positions).astype(F32).astype(BF16)


def normalize(values):
    center = values - jnp.mean(values, axis=-1, keepdims=True)
    spread = jnp.mean(center * center, axis=-1, keepdims=True)
    inverse_spread = lax.rsqrt(spread + EPSILON)
    return (center * inverse_spread, inverse_spread)


def enter_kernel(
    slot_ref, seg_ref, inc_ref, mod_ref, win_far, cot_ref, wo_far,
    packed_ref, rows_far, kv_far, qd_far,
    win_ref, wo_ref, rows_ref, kv_ref, qd_ref, sems,
):
    win_copy = pltpu.make_async_copy(win_far, win_ref, sems.at[0])
    wo_copy = pltpu.make_async_copy(wo_far, wo_ref, sems.at[1])
    rows_copy = pltpu.make_async_copy(rows_ref, rows_far, sems.at[2])
    kv_copy = pltpu.make_async_copy(kv_ref, kv_far, sems.at[3])
    qd_copy = pltpu.make_async_copy(qd_ref, qd_far, sems.at[4])
    win_copy.start()
    wo_copy.start()
    seg = seg_ref[...]
    packed = lax.dot_general(
        permutation(slot_ref[...]), inc_ref[...], LEFT, preferred_element_type=F32
    )
    packed_ref[...] = packed.astype(BF16)
    per_token = image_rows(seg, mod_ref[...])
    normed, _ = normalize(packed)
    hidden = (normed * (1.0 + per_token[:, D : 2 * D]) + per_token[:, :D]).astype(BF16)
    branch = (per_token[:, 2 * D :] * cot_ref[...].astype(F32)).astype(BF16)
    rows_ref[:, :D] = hidden
    rows_ref[:, D:] = branch
    rows_copy.start()
    win_copy.wait()
    turned = lax.dot_general(win_ref[...], hidden, LAST, preferred_element_type=F32)
    wo_copy.wait()
    back = lax.dot_general(wo_ref[...], branch, LAST, preferred_element_type=F32)
    spots = lax.broadcasted_iota(jnp.int32, (ROWS - HEAD, TOK), 0)
    ids = jnp.where(spots == 0, seg.astype(F32), 0.0)
    ones = jnp.where(spots <= 2, 1.0, 0.0)
    zeros = jnp.zeros((ROWS - HEAD, TOK), F32)
    for ref, copy, parts in (
        (kv_ref, kv_copy, ((turned, 1, ids), (turned, 2, ones))),
        (qd_ref, qd_copy, ((turned, 0, zeros), (back, 0, zeros))),
    ):
        for h in range(HEADS):
            for place, (table, part, pad) in enumerate(parts):
                first = part * ATT + h * HEAD
                block = jnp.concatenate([table[first : first + HEAD], pad], axis=0)
                ref[h, place * ROWS : (place + 1) * ROWS] = block.astype(BF16)
        copy.start()
    rows_copy.wait()
    kv_copy.wait()
    qd_copy.wait()


def attend_kernel(
    qd_ref, kv_ref, below_ref, above_ref, far_ref,
    own_ref, mine_ref, plus_ref, minus_ref, front_ref, rear_ref,
    k_s, v_s, kt_s, vt_s, q_s, p_s, dk_s, dv_s,
):
    spots = lax.broadcasted_iota(jnp.int32, (16, TOK), 0).astype(F32)
    blocks = [(ref, s) for ref in (kv_ref, below_ref, above_ref, far_ref) for s in range(PEERS)]
    for index, (ref, s) in enumerate(blocks):
        spot = pl.ds(index * TOK, TOK)
        keys = ref[s, 0:ROWS]
        values = ref[s, ROWS : 2 * ROWS]
        kt_s[:, spot] = keys
        vt_s[:, spot] = values
        ids = keys.astype(F32)[HEAD : HEAD + 1]
        same = spots == ids
        wide = jnp.concatenate(
            [keys.astype(F32), same.astype(F32), jnp.zeros((TOK - ROWS - 16, TOK), F32)], axis=0
        )
        k_s[spot, :] = wide.T.astype(BF16)
        wide = jnp.concatenate([values.astype(F32), jnp.zeros((TOK - ROWS, TOK), F32)], axis=0)
        v_s[spot, :] = wide.T.astype(BF16)
        if index < PEERS:
            q_s[0:ROWS, spot] = qd_ref[s, 0:ROWS]
            q_s[ROWS : ROWS + 16, spot] = jnp.where(same, 0.0, FAR).astype(BF16)
            q_s[ROWS + 16 : TOK, spot] = jnp.zeros((TOK - ROWS - 16, TOK), BF16)
            q_s[TOK:, spot] = qd_ref[s, ROWS : 2 * ROWS]
    dk_s[...] = jnp.zeros_like(dk_s)
    dv_s[...] = jnp.zeros_like(dv_s)

    def query_tile(block, carry):
        columns = pl.ds(pl.multiple_of(block * QUERY_TILE, QUERY_TILE), QUERY_TILE)
        queries = q_s[0:TOK, columns]

        def forward(tile, total):
            rows = pl.ds(pl.multiple_of(tile * KEY_TILE, KEY_TILE), KEY_TILE)
            powers = jnp.exp2(dot(k_s[rows, :], queries) * TO_BASE2).astype(BF16)
            p_s[rows, :] = powers
            return total + dot(vt_s[:, rows], powers)

        summed = lax.fori_loop(
            0, KEYS // KEY_TILE, forward, jnp.zeros((ROWS, QUERY_TILE), F32), unroll=8
        )
        totals = summed[HEAD : HEAD + 1]
        inverse = 1.0 / totals
        attended = (summed[0:HEAD] / totals).astype(BF16).astype(F32)
        cot = q_s[TOK:, columns]
        cot_wide = cot.astype(F32)
        delta = -jnp.sum(cot_wide[0:HEAD] * attended, axis=0, keepdims=True)
        high = delta.astype(BF16).astype(F32)
        middle = (delta - high).astype(BF16).astype(F32)
        low = delta - high - middle
        lines = lax.broadcasted_iota(jnp.int32, (ROWS - HEAD, QUERY_TILE), 0)
        pad = jnp.where(lines == 0, high, jnp.where(lines == 1, middle, jnp.where(lines == 2, low, 0.0)))
        shifted = jnp.concatenate(
            [cot_wide[0:HEAD], pad, jnp.zeros((TOK - ROWS, QUERY_TILE), F32)], axis=0
        ).astype(BF16)

        def backward(tile, total):
            rows = pl.ds(pl.multiple_of(tile * KEY_TILE, KEY_TILE), KEY_TILE)
            weights = p_s[rows, :].astype(F32) * inverse
            score = (weights * dot(v_s[rows, :], shifted)).astype(BF16)
            dk_s[:, rows] += lax.dot_general(
                queries[0:ROWS], score, LAST, preferred_element_type=F32
            )
            dv_s[:, rows] += lax.dot_general(
                cot, weights.astype(BF16), LAST, preferred_element_type=F32
            )
            return total + dot(kt_s[:, rows], score)

        dq = lax.fori_loop(
            0, KEYS // KEY_TILE, backward, jnp.zeros((ROWS, QUERY_TILE), F32), unroll=8
        )
        attended = jnp.concatenate([attended, jnp.zeros((ROWS - HEAD, QUERY_TILE), F32)], axis=0)
        dq = dq * FACTOR
        for part in range(QUERY_TILE // TOK):
            lanes = slice(part * TOK, (part + 1) * TOK)
            own_ref[block * (QUERY_TILE // TOK) + part, 0:ROWS] = attended[:, lanes].astype(BF16)
            own_ref[block * (QUERY_TILE // TOK) + part, ROWS : 2 * ROWS] = dq[:, lanes].astype(BF16)
        return carry

    lax.fori_loop(0, OWN // QUERY_TILE, query_tile, 0)
    blocks = [(ref, s) for ref in (mine_ref, minus_ref, plus_ref) for s in range(PEERS)]
    blocks += [(ref, s) for ref in (front_ref, rear_ref) for s in range(FRONT)]
    for index, (ref, s) in enumerate(blocks):
        spot = pl.ds(index * TOK, TOK)
        ref[s, 0:ROWS] = (dk_s[:, spot] * FACTOR).astype(BF16)
        ref[s, ROWS : 2 * ROWS] = dv_s[:, spot].astype(BF16)


def attend_call(queries, pairs, below, above, far):
    whole, half = shape(PEERS, 2 * ROWS, TOK), shape(FRONT, 2 * ROWS, TOK)
    return call(
        attend_kernel,
        (whole, whole, whole, whole, half, half),
        n_in=5,
        limit=36,
        flops=2 * 6 * OWN * KEYS * HEAD,
        scratch=(
            pltpu.VMEM((KEYS, TOK), BF16),
            pltpu.VMEM((KEYS, TOK), BF16),
            pltpu.VMEM((ROWS, KEYS), BF16),
            pltpu.VMEM((ROWS, KEYS), BF16),
            pltpu.VMEM((TOK + ROWS, OWN), BF16),
            pltpu.VMEM((KEYS, QUERY_TILE), BF16),
            pltpu.VMEM((ROWS, KEYS), F32),
            pltpu.VMEM((ROWS, KEYS), F32),
        ),
    )(queries, pairs, below, above, far)


def weights_kernel(
    r_ref, own_ref, mine_ref, first_ref, second_ref, rows_far,
    ret_ref, kept_ref, plus_ref, minus_ref, across_ref,
    rows_ref, sem,
):
    rows_copy = pltpu.make_async_copy(rows_far, rows_ref, sem)
    rows_copy.start()
    position = r_ref[0]
    for s in range(PEERS):
        both = mine_ref[s].astype(F32) + first_ref[s].astype(F32) + second_ref[s].astype(F32)
        ret_ref[s] = both.astype(BF16)

    def lined(ref, place):
        return jnp.concatenate(
            [ref[s, place * ROWS : (place + 1) * ROWS] for s in range(PEERS)], axis=1
        )

    rows_copy.wait()
    inner = jnp.concatenate([lined(own_ref, 1), lined(ret_ref, 0), lined(ret_ref, 1)], axis=0)
    inner = dot(inner, rows_ref[:, :D])
    outer = dot(lined(own_ref, 0), rows_ref[:, D:])
    for part in range(SETS):
        block = outer if part == 3 else inner[part * ROWS : (part + 1) * ROWS]
        block = block[:HEAD].astype(BF16)
        relative = (part - position) & 3

        @pl.when(relative == 0)
        def _():
            kept_ref[...] = block

        @pl.when(relative == 1)
        def _():
            plus_ref[...] = block

        @pl.when(relative == 3)
        def _():
            minus_ref[...] = block

        @pl.when(relative == 2)
        def _():
            across_ref[...] = block


def leave_kernel(slot_ref, seg_ref, own_ref, ret_ref, packed_ref, mod_ref, cot_ref, win_far, wo_far, out_ref, back_ref, win_ref, wo_ref, sems):
    win_copy = pltpu.make_async_copy(win_far, win_ref, sems.at[0])
    wo_copy = pltpu.make_async_copy(wo_far, wo_ref, sems.at[1])
    wo_copy.start()
    win_copy.start()

    def turned(ref, place):
        return [
            ref[h, place * ROWS : (place + 1) * ROWS].astype(F32)[0:HEAD] for h in range(HEADS)
        ]

    per_token = image_rows(seg_ref[...], mod_ref[...])
    scale = 1.0 + per_token[:, D : 2 * D]
    values = packed_ref[...].astype(F32)
    normed, inverse_spread = normalize(values)
    attended = jnp.concatenate(turned(own_ref, 0), axis=0).T.astype(BF16)
    wo_copy.wait()
    out_ref[...] = (values + per_token[:, 2 * D :] * dot(attended, wo_ref[...])).astype(BF16)
    cot = jnp.concatenate(turned(own_ref, 1) + turned(ret_ref, 0) + turned(ret_ref, 1), axis=0).T.astype(BF16)
    win_copy.wait()
    scaled = dot(cot, win_ref[...]) * scale
    packed_cot = cot_ref[...].astype(F32) + inverse_spread * (
        scaled
        - jnp.mean(scaled, axis=-1, keepdims=True)
        - normed * jnp.mean(scaled * normed, axis=-1, keepdims=True)
    )
    back_ref[...] = dot(permutation(slot_ref[...]), packed_cot.astype(BF16)).astype(BF16)


def shards(
    owned_patches,
    send_rows,
    receive_slot,
    segment_ids,
    class_label,
    drop_mask,
    class_table,
    modulation_weight,
    attention_in,
    attention_out,
    cotangent,
):
    slot, seg, cot = receive_slot[0], segment_ids, cotangent[0]
    spots = jnp.arange(TOK, dtype=jnp.int32)
    send_hot = send_rows[0, 0][:, None] == spots[None, :]
    outgoing = dot(send_hot.astype(BF16), owned_patches[0]).astype(BF16)
    class_label, outgoing = lax.optimization_barrier((class_label, outgoing))
    incoming = lax.all_to_all(
        outgoing.reshape(32, TOK // 32, D), "seq", split_axis=0, concat_axis=0, tiled=True
    ).reshape(TOK, D)
    chosen = jnp.where(drop_mask[0] == 1, CLASSES, class_label[0])
    condition = jnp.take(class_table, chosen, axis=0)
    activated = jax.nn.silu(condition.astype(F32)).astype(BF16)
    modulation = dot(activated, modulation_weight)
    turned_in = attention_in.T

    packed, rows, pairs, queries = call(
        enter_kernel,
        (
            shape(TOK, D),
            shape(TOK, 2 * D),
            shape(HEADS, 2 * ROWS, TOK),
            shape(HEADS, 2 * ROWS, TOK),
        ),
        n_in=7,
        limit=61,
        far_in=(4, 6),
        far_out=(1, 2, 3),
        scratch=(
            pltpu.VMEM((3 * ATT, D), BF16),
            pltpu.VMEM((ATT, D), BF16),
            pltpu.VMEM((TOK, 2 * D), BF16),
            pltpu.VMEM((HEADS, 2 * ROWS, TOK), BF16),
            pltpu.VMEM((HEADS, 2 * ROWS, TOK), BF16),
            pltpu.SemaphoreType.DMA((5,)),
        ),
        flops=2 * TOK * D * 4 * ATT,
    )(slot, seg, incoming, modulation, turned_in, cot, attention_out)
    all_rows = lax.all_gather(rows, "seq", axis_index_groups=HEAD_GROUPS, tiled=True)

    def trade(array):
        return lax.all_to_all(
            array, "seq", split_axis=0, concat_axis=0, axis_index_groups=HEAD_GROUPS, tiled=True
        )

    pairs = trade(pairs)
    pairs, queries = lax.optimization_barrier((pairs, queries))
    below = lax.ppermute(pairs, "seq", UP)
    above = lax.ppermute(pairs, "seq", DOWN)
    far = lax.ppermute(pairs, "seq", ACROSS)
    queries = trade(queries)

    own, mine, plus, minus, front, rear = attend_call(queries, pairs, below, above, far)

    def add(a, b):
        return (a.astype(F32) + b.astype(F32)).astype(BF16)

    ahead = lax.ppermute(front, "seq", UP)
    behind = lax.ppermute(rear, "seq", DOWN)
    plus = jnp.concatenate([add(plus[:FRONT], ahead), plus[FRONT:]], axis=0)
    minus = jnp.concatenate([minus[:FRONT], add(minus[FRONT:], behind)], axis=0)
    first = lax.ppermute(plus, "seq", UP)
    second = lax.ppermute(minus, "seq", DOWN)
    local = own
    own = trade(own)
    position = (lax.axis_index("seq") // PEERS).astype(jnp.int32).reshape(1)
    part = shape(HEAD, D)
    returning, kept, plus, minus, across = call(
        weights_kernel,
        (shape(PEERS, 2 * ROWS, TOK), part, part, part, part),
        smem=1,
        n_in=6,
        limit=60,
        far_in=(5,),
        scratch=(pltpu.VMEM((OWN, 2 * D), BF16), pltpu.SemaphoreType.DMA),
        flops=2 * 4 * ROWS * OWN * D,
    )(position, local, mine, first, second, all_rows)

    piece = kept.astype(F32)
    for block, hop in ((plus, UP), (minus, DOWN), (across, ACROSS)):
        piece = piece + lax.ppermute(block, "seq", hop).astype(F32)
    piece = piece.astype(BF16)
    others = [
        lax.ppermute(piece, "grp", [(i, (i + k) % 4) for i in range(4)]) for k in (1, 3, 2)
    ]
    norm_factor = (4 * 32 * TOK) ** (-0.5)
    summed = piece.astype(F32)
    for other in others:
        summed = summed + other.astype(F32)
    summed = (summed * norm_factor).astype(BF16)
    summed, returning = lax.optimization_barrier((summed, returning))
    gathered = lax.all_gather(summed, "seq", tiled=True)
    gradient_in = gathered[: 3 * ATT].T
    gradient_out = gathered[3 * ATT :]

    returned = trade(returning)
    layer_output, back_order = call(
        leave_kernel,
        (shape(TOK, D), shape(TOK, D)),
        n_in=9,
        limit=61,
        far_in=(7, 8),
        scratch=(
            pltpu.VMEM((3 * ATT, D), BF16),
            pltpu.VMEM((ATT, D), BF16),
            pltpu.SemaphoreType.DMA((2,)),
        ),
        flops=2 * TOK * D * 4 * ATT,
    )(slot, seg, own, returned, packed, modulation, cot, turned_in, attention_out)
    home = lax.all_to_all(
        back_order.reshape(32, TOK // 32, D), "seq", split_axis=0, concat_axis=0, tiled=True
    ).reshape(TOK, D)
    home_hot = spots[:, None] == send_rows[0, 0][None, :]
    owner_gradient = dot(home_hot.astype(BF16), home).astype(BF16)
    return (layer_output[None], owner_gradient[None], gradient_in, gradient_out)


def solution(mesh):
    return jax.shard_map(
        shards,
        mesh=mesh,
        in_specs=(
            P("grp", "seq", None),
            P("grp", "seq", None),
            P("grp", "seq", None),
            P("grp", "seq"),
            P("grp", None),
            P("grp", None),
            P(),
            P(),
            P(),
            P(),
            P("grp", "seq", None),
        ),
        out_specs=(P("grp", "seq", None), P("grp", "seq", None), P(), P()),
        check_vma=False,
    )
```

```python
import math

import jax
import jax.numpy as jnp
from jax import lax
from jax.experimental import pallas as pl
from jax.experimental.pallas import tpu as pltpu
from jax.sharding import PartitionSpec as P

HEADS = 8
CLASSES = 1000
EPSILON = 1e-06

D = 1152
ATT = 576
HEAD = 72
ROWS = 80
TOK = 128
SETS = 4
PEERS = 8
OWN = PEERS * TOK
KEYS = SETS * OWN
QUERY_TILE = 1024
KEY_TILE = 512
FAR = -1e30

F32 = jnp.float32
BF16 = jnp.bfloat16
FACTOR = HEAD ** (-0.5)
TO_BASE2 = FACTOR * math.log2(math.e)

HEAD_GROUPS = [[PEERS * r + h for h in range(PEERS)] for r in range(SETS)]
UP = [(i, (i + PEERS) % 32) for i in range(32)]
DOWN = [(i, (i - PEERS) % 32) for i in range(32)]
ACROSS = [(i, (i + 2 * PEERS) % 32) for i in range(32)]
FRONT = PEERS // 2

LEFT = (((0,), (0,)), ((), ()))
LAST = (((1,), (1,)), ((), ()))


def dot(a, b):
    return jnp.dot(a, b, preferred_element_type=F32)


def call(kernel, outs, scratch=(), flops=0, smem=0, n_in=1, limit=20, far_in=(), far_out=()):
    vmem = pl.BlockSpec(memory_space=pltpu.VMEM)
    scalar = pl.BlockSpec(memory_space=pltpu.SMEM)
    hbm = pl.BlockSpec(memory_space=pltpu.MemorySpace.HBM)
    return pl.pallas_call(
        kernel,
        out_shape=outs,
        in_specs=[scalar] * smem + [hbm if i in far_in else vmem for i in range(smem, n_in)],
        out_specs=[hbm if i in far_out else vmem for i in range(len(outs))],
        scratch_shapes=list(scratch),
        compiler_params=pltpu.CompilerParams(vmem_limit_bytes=limit * 1024 * 1024),
        cost_estimate=pl.CostEstimate(flops=flops, bytes_accessed=4_000_000, transcendentals=0),
    )


def shape(*dims):
    return jax.ShapeDtypeStruct(dims, BF16)


def image_rows(seg, table):
    spots = lax.broadcasted_iota(jnp.int32, (16, TOK), 0)
    one_hot = (spots == seg).astype(F32)
    return lax.dot_general(
        one_hot, table, LEFT, precision=lax.Precision.HIGHEST, preferred_element_type=F32
    )


def permutation(positions):
    spots = lax.broadcasted_iota(jnp.int32, (TOK, TOK), 0)
    return (spots == positions).astype(F32).astype(BF16)


def normalize(values):
    center = values - jnp.mean(values, axis=-1, keepdims=True)
    spread = jnp.mean(center * center, axis=-1, keepdims=True)
    inverse_spread = lax.rsqrt(spread + EPSILON)
    return (center * inverse_spread, inverse_spread)


def enter_kernel(
    slot_ref, seg_ref, inc_ref, mod_ref, win_far, cot_ref, wo_far,
    packed_ref, rows_far, kv_far, qd_far,
    win_ref, wo_ref, rows_ref, kv_ref, qd_ref, sems,
):
    win_copy = pltpu.make_async_copy(win_far, win_ref, sems.at[0])
    wo_copy = pltpu.make_async_copy(wo_far, wo_ref, sems.at[1])
    rows_copy = pltpu.make_async_copy(rows_ref, rows_far, sems.at[2])
    kv_copy = pltpu.make_async_copy(kv_ref, kv_far, sems.at[3])
    qd_copy = pltpu.make_async_copy(qd_ref, qd_far, sems.at[4])
    win_copy.start()
    wo_copy.start()
    seg = seg_ref[...]
    packed = lax.dot_general(
        permutation(slot_ref[...]), inc_ref[...], LEFT, preferred_element_type=F32
    )
    packed_ref[...] = packed.astype(BF16)
    per_token = image_rows(seg, mod_ref[...])
    normed, _ = normalize(packed)
    hidden = (normed * (1.0 + per_token[:, D : 2 * D]) + per_token[:, :D]).astype(BF16)
    branch = (per_token[:, 2 * D :] * cot_ref[...].astype(F32)).astype(BF16)
    rows_ref[:, :D] = hidden
    rows_ref[:, D:] = branch
    rows_copy.start()
    win_copy.wait()
    turned = lax.dot_general(win_ref[...], hidden, LAST, preferred_element_type=F32)
    wo_copy.wait()
    back = lax.dot_general(wo_ref[...], branch, LAST, preferred_element_type=F32)
    spots = lax.broadcasted_iota(jnp.int32, (ROWS - HEAD, TOK), 0)
    ids = jnp.where(spots == 0, seg.astype(F32), 0.0)
    ones = jnp.where(spots <= 2, 1.0, 0.0)
    zeros = jnp.zeros((ROWS - HEAD, TOK), F32)
    for ref, copy, parts in (
        (kv_ref, kv_copy, ((turned, 1, ids), (turned, 2, ones))),
        (qd_ref, qd_copy, ((turned, 0, zeros), (back, 0, zeros))),
    ):
        for h in range(HEADS):
            for place, (table, part, pad) in enumerate(parts):
                first = part * ATT + h * HEAD
                block = jnp.concatenate([table[first : first + HEAD], pad], axis=0)
                ref[h, place * ROWS : (place + 1) * ROWS] = block.astype(BF16)
        copy.start()
    rows_copy.wait()
    kv_copy.wait()
    qd_copy.wait()


def attend_kernel(
    qd_ref, kv_ref, below_ref, above_ref, far_ref,
    own_ref, mine_ref, plus_ref, minus_ref, front_ref, rear_ref,
    k_s, v_s, kt_s, vt_s, q_s, p_s, dk_s, dv_s,
):
    spots = lax.broadcasted_iota(jnp.int32, (16, TOK), 0).astype(F32)
    blocks = [(ref, s) for ref in (kv_ref, below_ref, above_ref, far_ref) for s in range(PEERS)]
    for index, (ref, s) in enumerate(blocks):
        spot = pl.ds(index * TOK, TOK)
        keys = ref[s, 0:ROWS]
        values = ref[s, ROWS : 2 * ROWS]
        kt_s[:, spot] = keys
        vt_s[:, spot] = values
        ids = keys.astype(F32)[HEAD : HEAD + 1]
        same = spots == ids
        wide = jnp.concatenate(
            [keys.astype(F32), same.astype(F32), jnp.zeros((TOK - ROWS - 16, TOK), F32)], axis=0
        )
        k_s[spot, :] = wide.T.astype(BF16)
        wide = jnp.concatenate([values.astype(F32), jnp.zeros((TOK - ROWS, TOK), F32)], axis=0)
        v_s[spot, :] = wide.T.astype(BF16)
        if index < PEERS:
            q_s[0:ROWS, spot] = qd_ref[s, 0:ROWS]
            q_s[ROWS : ROWS + 16, spot] = jnp.where(same, 0.0, FAR).astype(BF16)
            q_s[ROWS + 16 : TOK, spot] = jnp.zeros((TOK - ROWS - 16, TOK), BF16)
            q_s[TOK:, spot] = qd_ref[s, ROWS : 2 * ROWS]
    dk_s[...] = jnp.zeros_like(dk_s)
    dv_s[...] = jnp.zeros_like(dv_s)

    def query_tile(block, carry):
        columns = pl.ds(pl.multiple_of(block * QUERY_TILE, QUERY_TILE), QUERY_TILE)
        queries = q_s[0:TOK, columns]

        def forward(tile, total):
            rows = pl.ds(pl.multiple_of(tile * KEY_TILE, KEY_TILE), KEY_TILE)
            powers = jnp.exp2(dot(k_s[rows, :], queries) * TO_BASE2).astype(BF16)
            p_s[rows, :] = powers
            return total + dot(vt_s[:, rows], powers)

        summed = lax.fori_loop(
            0, KEYS // KEY_TILE, forward, jnp.zeros((ROWS, QUERY_TILE), F32), unroll=8
        )
        totals = summed[HEAD : HEAD + 1]
        inverse = 1.0 / totals
        attended = (summed[0:HEAD] / totals).astype(BF16).astype(F32)
        cot = q_s[TOK:, columns]
        cot_wide = cot.astype(F32)
        delta = -jnp.sum(cot_wide[0:HEAD] * attended, axis=0, keepdims=True)
        high = delta.astype(BF16).astype(F32)
        middle = (delta - high).astype(BF16).astype(F32)
        low = delta - high - middle
        lines = lax.broadcasted_iota(jnp.int32, (ROWS - HEAD, QUERY_TILE), 0)
        pad = jnp.where(lines == 0, high, jnp.where(lines == 1, middle, jnp.where(lines == 2, low, 0.0)))
        shifted = jnp.concatenate(
            [cot_wide[0:HEAD], pad, jnp.zeros((TOK - ROWS, QUERY_TILE), F32)], axis=0
        ).astype(BF16)

        def backward(tile, total):
            rows = pl.ds(pl.multiple_of(tile * KEY_TILE, KEY_TILE), KEY_TILE)
            weights = p_s[rows, :].astype(F32) * inverse
            score = (weights * dot(v_s[rows, :], shifted)).astype(BF16)
            dk_s[:, rows] += lax.dot_general(
                queries[0:ROWS], score, LAST, preferred_element_type=F32
            )
            dv_s[:, rows] += lax.dot_general(
                cot, weights.astype(BF16), LAST, preferred_element_type=F32
            )
            return total + dot(kt_s[:, rows], score)

        dq = lax.fori_loop(
            0, KEYS // KEY_TILE, backward, jnp.zeros((ROWS, QUERY_TILE), F32), unroll=8
        )
        attended = jnp.concatenate([attended, jnp.zeros((ROWS - HEAD, QUERY_TILE), F32)], axis=0)
        dq = dq * FACTOR
        for part in range(QUERY_TILE // TOK):
            lanes = slice(part * TOK, (part + 1) * TOK)
            own_ref[block * (QUERY_TILE // TOK) + part, 0:ROWS] = attended[:, lanes].astype(BF16)
            own_ref[block * (QUERY_TILE // TOK) + part, ROWS : 2 * ROWS] = dq[:, lanes].astype(BF16)
        return carry

    lax.fori_loop(0, OWN // QUERY_TILE, query_tile, 0)
    blocks = [(ref, s) for ref in (mine_ref, minus_ref, plus_ref) for s in range(PEERS)]
    blocks += [(ref, s) for ref in (front_ref, rear_ref) for s in range(FRONT)]
    for index, (ref, s) in enumerate(blocks):
        spot = pl.ds(index * TOK, TOK)
        ref[s, 0:ROWS] = (dk_s[:, spot] * FACTOR).astype(BF16)
        ref[s, ROWS : 2 * ROWS] = dv_s[:, spot].astype(BF16)


def attend_call(queries, pairs, below, above, far):
    whole, half = shape(PEERS, 2 * ROWS, TOK), shape(FRONT, 2 * ROWS, TOK)
    return call(
        attend_kernel,
        (whole, whole, whole, whole, half, half),
        n_in=5,
        limit=36,
        flops=2 * 6 * OWN * KEYS * HEAD,
        scratch=(
            pltpu.VMEM((KEYS, TOK), BF16),
            pltpu.VMEM((KEYS, TOK), BF16),
            pltpu.VMEM((ROWS, KEYS), BF16),
            pltpu.VMEM((ROWS, KEYS), BF16),
            pltpu.VMEM((TOK + ROWS, OWN), BF16),
            pltpu.VMEM((KEYS, QUERY_TILE), BF16),
            pltpu.VMEM((ROWS, KEYS), F32),
            pltpu.VMEM((ROWS, KEYS), F32),
        ),
    )(queries, pairs, below, above, far)


def lined(ref, place):
    return jnp.concatenate(
        [ref[s, place * ROWS : (place + 1) * ROWS] for s in range(PEERS)], axis=1
    )


def query_weights_kernel(own_ref, rows_ref, query_ref, out_ref):
    query_ref[...] = dot(lined(own_ref, 1), rows_ref[:, :D])[:HEAD].astype(BF16)
    out_ref[...] = dot(lined(own_ref, 0), rows_ref[:, D:])[:HEAD].astype(BF16)


def weights_kernel(
    r_ref, query_ref, out_ref, own_ref, mine_ref, first_ref, second_ref, rows_ref,
    ret_ref, kept_ref, plus_ref, minus_ref, across_ref,
):
    position = r_ref[0]
    for s in range(PEERS):
        both = mine_ref[s].astype(F32) + first_ref[s].astype(F32) + second_ref[s].astype(F32)
        ret_ref[s, : 2 * ROWS] = own_ref[s]
        ret_ref[s, 2 * ROWS :] = both.astype(BF16)
    inner = jnp.concatenate([lined(ret_ref, 2), lined(ret_ref, 3)], axis=0)
    inner = dot(inner, rows_ref[:, :D])
    for part in range(SETS):
        for step, ref in enumerate((kept_ref, plus_ref, across_ref, minus_ref)):

            @pl.when(((part - position) & 3) == step)
            def _():
                if part == 0:
                    ref[...] = query_ref[...]
                elif part == 3:
                    ref[...] = out_ref[...]
                else:
                    first = (part - 1) * ROWS
                    ref[...] = inner[first : first + HEAD].astype(BF16)


def leave_kernel(slot_ref, seg_ref, ret_ref, packed_ref, mod_ref, cot_ref, win_far, wo_far, out_ref, back_ref, win_ref, wo_ref, sems):
    win_copy = pltpu.make_async_copy(win_far, win_ref, sems.at[0])
    wo_copy = pltpu.make_async_copy(wo_far, wo_ref, sems.at[1])
    wo_copy.start()
    win_copy.start()

    def turned(place):
        return [
            ret_ref[h, place * ROWS : (place + 1) * ROWS].astype(F32)[0:HEAD] for h in range(HEADS)
        ]

    per_token = image_rows(seg_ref[...], mod_ref[...])
    scale = 1.0 + per_token[:, D : 2 * D]
    values = packed_ref[...].astype(F32)
    normed, inverse_spread = normalize(values)
    attended = jnp.concatenate(turned(0), axis=0).T.astype(BF16)
    wo_copy.wait()
    out_ref[...] = (values + per_token[:, 2 * D :] * dot(attended, wo_ref[...])).astype(BF16)
    cot = jnp.concatenate(turned(1) + turned(2) + turned(3), axis=0).T.astype(BF16)
    win_copy.wait()
    scaled = dot(cot, win_ref[...]) * scale
    packed_cot = cot_ref[...].astype(F32) + inverse_spread * (
        scaled
        - jnp.mean(scaled, axis=-1, keepdims=True)
        - normed * jnp.mean(scaled * normed, axis=-1, keepdims=True)
    )
    back_ref[...] = dot(permutation(slot_ref[...]), packed_cot.astype(BF16)).astype(BF16)


def shards(
    owned_patches,
    send_rows,
    receive_slot,
    segment_ids,
    class_label,
    drop_mask,
    class_table,
    modulation_weight,
    attention_in,
    attention_out,
    cotangent,
):
    slot, seg, cot = receive_slot[0], segment_ids, cotangent[0]
    spots = jnp.arange(TOK, dtype=jnp.int32)
    send_hot = send_rows[0, 0][:, None] == spots[None, :]
    outgoing = dot(send_hot.astype(BF16), owned_patches[0]).astype(BF16)
    class_label, outgoing = lax.optimization_barrier((class_label, outgoing))
    incoming = lax.all_to_all(
        outgoing.reshape(32, TOK // 32, D), "seq", split_axis=0, concat_axis=0, tiled=True
    ).reshape(TOK, D)
    chosen = jnp.where(drop_mask[0] == 1, CLASSES, class_label[0])
    condition = jnp.take(class_table, chosen, axis=0)
    activated = jax.nn.silu(condition.astype(F32)).astype(BF16)
    modulation = dot(activated, modulation_weight)
    turned_in = attention_in.T

    packed, rows, pairs, queries = call(
        enter_kernel,
        (
            shape(TOK, D),
            shape(TOK, 2 * D),
            shape(HEADS, 2 * ROWS, TOK),
            shape(HEADS, 2 * ROWS, TOK),
        ),
        n_in=7,
        limit=61,
        far_in=(4, 6),
        far_out=(1, 2, 3),
        scratch=(
            pltpu.VMEM((3 * ATT, D), BF16),
            pltpu.VMEM((ATT, D), BF16),
            pltpu.VMEM((TOK, 2 * D), BF16),
            pltpu.VMEM((HEADS, 2 * ROWS, TOK), BF16),
            pltpu.VMEM((HEADS, 2 * ROWS, TOK), BF16),
            pltpu.SemaphoreType.DMA((5,)),
        ),
        flops=2 * TOK * D * 4 * ATT,
    )(slot, seg, incoming, modulation, turned_in, cot, attention_out)
    all_rows = lax.all_gather(rows, "seq", axis_index_groups=HEAD_GROUPS, tiled=True)

    def trade(array):
        return lax.all_to_all(
            array, "seq", split_axis=0, concat_axis=0, axis_index_groups=HEAD_GROUPS, tiled=True
        )

    pairs = trade(pairs)
    pairs, queries = lax.optimization_barrier((pairs, queries))
    below = lax.ppermute(pairs, "seq", UP)
    above = lax.ppermute(pairs, "seq", DOWN)
    far = lax.ppermute(pairs, "seq", ACROSS)
    queries = trade(queries)

    own, mine, plus, minus, front, rear = attend_call(queries, pairs, below, above, far)

    def add(a, b):
        return (a.astype(F32) + b.astype(F32)).astype(BF16)

    ahead = lax.ppermute(front, "seq", UP)
    behind = lax.ppermute(rear, "seq", DOWN)
    plus = jnp.concatenate([add(plus[:FRONT], ahead), plus[FRONT:]], axis=0)
    minus = jnp.concatenate([minus[:FRONT], add(minus[FRONT:], behind)], axis=0)
    first = lax.ppermute(plus, "seq", UP)
    second = lax.ppermute(minus, "seq", DOWN)
    position = (lax.axis_index("seq") // PEERS).astype(jnp.int32).reshape(1)
    part = shape(HEAD, D)
    query_part, out_part = call(
        query_weights_kernel,
        (part, part),
        n_in=2,
        limit=16,
        flops=2 * 2 * ROWS * OWN * D,
    )(own, all_rows)
    returning, kept, plus, minus, across = call(
        weights_kernel,
        (shape(PEERS, 4 * ROWS, TOK), part, part, part, part),
        smem=1,
        n_in=8,
        limit=16,
        flops=2 * 2 * ROWS * OWN * D,
    )(position, query_part, out_part, own, mine, first, second, all_rows)

    piece = kept.astype(F32)
    for block, hop in ((plus, UP), (minus, DOWN), (across, ACROSS)):
        piece = piece + lax.ppermute(block, "seq", hop).astype(F32)
    piece = piece.astype(BF16)
    others = [
        lax.ppermute(piece, "grp", [(i, (i + k) % 4) for i in range(4)]) for k in (1, 3, 2)
    ]
    norm_factor = (4 * 32 * TOK) ** (-0.5)
    summed = piece.astype(F32)
    for other in others:
        summed = summed + other.astype(F32)
    summed = (summed * norm_factor).astype(BF16)
    summed, returning = lax.optimization_barrier((summed, returning))
    gathered = lax.all_gather(summed, "seq", tiled=True)
    gradient_in = gathered[: 3 * ATT].T
    gradient_out = gathered[3 * ATT :]

    returned = trade(returning)
    layer_output, back_order = call(
        leave_kernel,
        (shape(TOK, D), shape(TOK, D)),
        n_in=8,
        limit=61,
        far_in=(6, 7),
        scratch=(
            pltpu.VMEM((3 * ATT, D), BF16),
            pltpu.VMEM((ATT, D), BF16),
            pltpu.SemaphoreType.DMA((2,)),
        ),
        flops=2 * TOK * D * 4 * ATT,
    )(slot, seg, returned, packed, modulation, cot, turned_in, attention_out)
    home = lax.all_to_all(
        back_order.reshape(32, TOK // 32, D), "seq", split_axis=0, concat_axis=0, tiled=True
    ).reshape(TOK, D)
    home_hot = spots[:, None] == send_rows[0, 0][None, :]
    owner_gradient = dot(home_hot.astype(BF16), home).astype(BF16)
    return (layer_output[None], owner_gradient[None], gradient_in, gradient_out)


def solution(mesh):
    return jax.shard_map(
        shards,
        mesh=mesh,
        in_specs=(
            P("grp", "seq", None),
            P("grp", "seq", None),
            P("grp", "seq", None),
            P("grp", "seq"),
            P("grp", None),
            P("grp", None),
            P(),
            P(),
            P(),
            P(),
            P("grp", "seq", None),
        ),
        out_specs=(P("grp", "seq", None), P("grp", "seq", None), P(), P()),
        check_vma=False,
    )
```

```python
import math

import jax
import jax.numpy as jnp
from jax import lax
from jax.experimental import pallas as pl
from jax.experimental.pallas import tpu as pltpu
from jax.sharding import PartitionSpec as P

HEADS = 8
CLASSES = 1000
EPSILON = 1e-06

D = 1152
ATT = 576
HEAD = 72
ROWS = 80
TOK = 128
SETS = 4
PEERS = 8
OWN = PEERS * TOK
KEYS = SETS * OWN
QUERY_TILE = 1024
KEY_TILE = 512
FAR = -1e30

F32 = jnp.float32
BF16 = jnp.bfloat16
FACTOR = HEAD ** (-0.5)
TO_BASE2 = FACTOR * math.log2(math.e)

HEAD_GROUPS = [[PEERS * r + h for h in range(PEERS)] for r in range(SETS)]
UP = [(i, (i + PEERS) % 32) for i in range(32)]
DOWN = [(i, (i - PEERS) % 32) for i in range(32)]
ACROSS = [(i, (i + 2 * PEERS) % 32) for i in range(32)]
FRONT = PEERS // 2

LEFT = (((0,), (0,)), ((), ()))
LAST = (((1,), (1,)), ((), ()))


def dot(a, b):
    return jnp.dot(a, b, preferred_element_type=F32)


def call(kernel, outs, scratch=(), flops=0, smem=0, n_in=1, limit=20, far_in=(), far_out=()):
    vmem = pl.BlockSpec(memory_space=pltpu.VMEM)
    scalar = pl.BlockSpec(memory_space=pltpu.SMEM)
    hbm = pl.BlockSpec(memory_space=pltpu.MemorySpace.HBM)
    return pl.pallas_call(
        kernel,
        out_shape=outs,
        in_specs=[scalar] * smem + [hbm if i in far_in else vmem for i in range(smem, n_in)],
        out_specs=[hbm if i in far_out else vmem for i in range(len(outs))],
        scratch_shapes=list(scratch),
        compiler_params=pltpu.CompilerParams(vmem_limit_bytes=limit * 1024 * 1024),
        cost_estimate=pl.CostEstimate(flops=flops, bytes_accessed=4_000_000, transcendentals=0),
    )


def shape(*dims):
    return jax.ShapeDtypeStruct(dims, BF16)


def image_rows(seg, table):
    spots = lax.broadcasted_iota(jnp.int32, (16, TOK), 0)
    one_hot = (spots == seg).astype(F32)
    return lax.dot_general(
        one_hot, table, LEFT, precision=lax.Precision.HIGHEST, preferred_element_type=F32
    )


def permutation(positions):
    spots = lax.broadcasted_iota(jnp.int32, (TOK, TOK), 0)
    return (spots == positions).astype(F32).astype(BF16)


def normalize(values):
    center = values - jnp.mean(values, axis=-1, keepdims=True)
    spread = jnp.mean(center * center, axis=-1, keepdims=True)
    inverse_spread = lax.rsqrt(spread + EPSILON)
    return (center * inverse_spread, inverse_spread)


def enter_kernel(
    slot_ref, seg_ref, inc_ref, mod_ref, win_far, cot_ref, wo_far,
    packed_ref, rows_far, kv_far, qd_far,
    win_ref, wo_ref, rows_ref, kv_ref, qd_ref, sems,
):
    win_copy = pltpu.make_async_copy(win_far, win_ref, sems.at[0])
    wo_copy = pltpu.make_async_copy(wo_far, wo_ref, sems.at[1])
    rows_copy = pltpu.make_async_copy(rows_ref, rows_far, sems.at[2])
    kv_copy = pltpu.make_async_copy(kv_ref, kv_far, sems.at[3])
    qd_copy = pltpu.make_async_copy(qd_ref, qd_far, sems.at[4])
    win_copy.start()
    wo_copy.start()
    seg = seg_ref[...]
    packed = lax.dot_general(
        permutation(slot_ref[...]), inc_ref[...], LEFT, preferred_element_type=F32
    )
    packed_ref[...] = packed.astype(BF16)
    per_token = image_rows(seg, mod_ref[...])
    normed, _ = normalize(packed)
    hidden = (normed * (1.0 + per_token[:, D : 2 * D]) + per_token[:, :D]).astype(BF16)
    branch = (per_token[:, 2 * D :] * cot_ref[...].astype(F32)).astype(BF16)
    rows_ref[:, :D] = hidden
    rows_ref[:, D:] = branch
    rows_copy.start()
    win_copy.wait()
    turned = lax.dot_general(win_ref[...], hidden, LAST, preferred_element_type=F32)
    wo_copy.wait()
    back = lax.dot_general(wo_ref[...], branch, LAST, preferred_element_type=F32)
    spots = lax.broadcasted_iota(jnp.int32, (ROWS - HEAD, TOK), 0)
    ids = jnp.where(spots == 0, seg.astype(F32), 0.0)
    ones = jnp.where(spots <= 2, 1.0, 0.0)
    zeros = jnp.zeros((ROWS - HEAD, TOK), F32)
    for ref, copy, parts in (
        (kv_ref, kv_copy, ((turned, 1, ids), (turned, 2, ones))),
        (qd_ref, qd_copy, ((turned, 0, zeros), (back, 0, zeros))),
    ):
        for h in range(HEADS):
            for place, (table, part, pad) in enumerate(parts):
                first = part * ATT + h * HEAD
                block = jnp.concatenate([table[first : first + HEAD], pad], axis=0)
                ref[h, place * ROWS : (place + 1) * ROWS] = block.astype(BF16)
        copy.start()
    rows_copy.wait()
    kv_copy.wait()
    qd_copy.wait()


def attend_kernel(
    qd_ref, kv_ref, below_ref, above_ref, far_ref,
    own_ref, mine_ref, plus_ref, minus_ref, front_ref, rear_ref,
    k_s, v_s, kt_s, vt_s, q_s, p_s, dk_s, dv_s,
):
    spots = lax.broadcasted_iota(jnp.int32, (16, TOK), 0).astype(F32)
    blocks = [(ref, s) for ref in (kv_ref, below_ref, above_ref, far_ref) for s in range(PEERS)]
    for index, (ref, s) in enumerate(blocks):
        spot = pl.ds(index * TOK, TOK)
        keys = ref[s, 0:ROWS]
        values = ref[s, ROWS : 2 * ROWS]
        kt_s[:, spot] = keys
        vt_s[:, spot] = values
        ids = keys.astype(F32)[HEAD : HEAD + 1]
        same = spots == ids
        wide = jnp.concatenate(
            [keys.astype(F32), same.astype(F32), jnp.zeros((TOK - ROWS - 16, TOK), F32)], axis=0
        )
        k_s[spot, :] = wide.T.astype(BF16)
        wide = jnp.concatenate([values.astype(F32), jnp.zeros((TOK - ROWS, TOK), F32)], axis=0)
        v_s[spot, :] = wide.T.astype(BF16)
        if index < PEERS:
            q_s[0:ROWS, spot] = qd_ref[s, 0:ROWS]
            q_s[ROWS : ROWS + 16, spot] = jnp.where(same, 0.0, FAR).astype(BF16)
            q_s[ROWS + 16 : TOK, spot] = jnp.zeros((TOK - ROWS - 16, TOK), BF16)
            q_s[TOK:, spot] = qd_ref[s, ROWS : 2 * ROWS]
    dk_s[...] = jnp.zeros_like(dk_s)
    dv_s[...] = jnp.zeros_like(dv_s)

    def query_tile(block, carry):
        columns = pl.ds(pl.multiple_of(block * QUERY_TILE, QUERY_TILE), QUERY_TILE)
        queries = q_s[0:TOK, columns]

        def forward(tile, total):
            rows = pl.ds(pl.multiple_of(tile * KEY_TILE, KEY_TILE), KEY_TILE)
            powers = jnp.exp2(dot(k_s[rows, :], queries) * TO_BASE2).astype(BF16)
            p_s[rows, :] = powers
            return total + dot(vt_s[:, rows], powers)

        summed = lax.fori_loop(
            0, KEYS // KEY_TILE, forward, jnp.zeros((ROWS, QUERY_TILE), F32), unroll=8
        )
        totals = summed[HEAD : HEAD + 1]
        inverse = 1.0 / totals
        attended = (summed[0:HEAD] / totals).astype(BF16).astype(F32)
        cot = q_s[TOK:, columns]
        cot_wide = cot.astype(F32)
        delta = -jnp.sum(cot_wide[0:HEAD] * attended, axis=0, keepdims=True)
        high = delta.astype(BF16).astype(F32)
        middle = (delta - high).astype(BF16).astype(F32)
        low = delta - high - middle
        lines = lax.broadcasted_iota(jnp.int32, (ROWS - HEAD, QUERY_TILE), 0)
        pad = jnp.where(lines == 0, high, jnp.where(lines == 1, middle, jnp.where(lines == 2, low, 0.0)))
        shifted = jnp.concatenate(
            [cot_wide[0:HEAD], pad, jnp.zeros((TOK - ROWS, QUERY_TILE), F32)], axis=0
        ).astype(BF16)

        def backward(tile, total):
            rows = pl.ds(pl.multiple_of(tile * KEY_TILE, KEY_TILE), KEY_TILE)
            weights = p_s[rows, :].astype(F32) * inverse
            score = (weights * dot(v_s[rows, :], shifted)).astype(BF16)
            dk_s[:, rows] += lax.dot_general(
                queries[0:ROWS], score, LAST, preferred_element_type=F32
            )
            dv_s[:, rows] += lax.dot_general(
                cot, weights.astype(BF16), LAST, preferred_element_type=F32
            )
            return total + dot(kt_s[:, rows], score)

        dq = lax.fori_loop(
            0, KEYS // KEY_TILE, backward, jnp.zeros((ROWS, QUERY_TILE), F32), unroll=8
        )
        attended = jnp.concatenate([attended, jnp.zeros((ROWS - HEAD, QUERY_TILE), F32)], axis=0)
        dq = dq * FACTOR
        for part in range(QUERY_TILE // TOK):
            lanes = slice(part * TOK, (part + 1) * TOK)
            own_ref[block * (QUERY_TILE // TOK) + part, 0:ROWS] = attended[:, lanes].astype(BF16)
            own_ref[block * (QUERY_TILE // TOK) + part, ROWS : 2 * ROWS] = dq[:, lanes].astype(BF16)
        return carry

    lax.fori_loop(0, OWN // QUERY_TILE, query_tile, 0)
    blocks = [(ref, s) for ref in (mine_ref, minus_ref, plus_ref) for s in range(PEERS)]
    blocks += [(ref, s) for ref in (front_ref, rear_ref) for s in range(FRONT)]
    for index, (ref, s) in enumerate(blocks):
        spot = pl.ds(index * TOK, TOK)
        ref[s, 0:ROWS] = (dk_s[:, spot] * FACTOR).astype(BF16)
        ref[s, ROWS : 2 * ROWS] = dv_s[:, spot].astype(BF16)


def attend_call(queries, pairs, below, above, far):
    whole, half = shape(PEERS, 2 * ROWS, TOK), shape(FRONT, 2 * ROWS, TOK)
    return call(
        attend_kernel,
        (whole, whole, whole, whole, half, half),
        n_in=5,
        limit=36,
        flops=2 * 6 * OWN * KEYS * HEAD,
        scratch=(
            pltpu.VMEM((KEYS, TOK), BF16),
            pltpu.VMEM((KEYS, TOK), BF16),
            pltpu.VMEM((ROWS, KEYS), BF16),
            pltpu.VMEM((ROWS, KEYS), BF16),
            pltpu.VMEM((TOK + ROWS, OWN), BF16),
            pltpu.VMEM((KEYS, QUERY_TILE), BF16),
            pltpu.VMEM((ROWS, KEYS), F32),
            pltpu.VMEM((ROWS, KEYS), F32),
        ),
    )(queries, pairs, below, above, far)


def lined(ref, place):
    return jnp.concatenate(
        [ref[s, place * ROWS : (place + 1) * ROWS] for s in range(PEERS)], axis=1
    )


def query_weights_kernel(own_ref, rows_ref, query_ref, out_ref):
    query_ref[...] = dot(lined(own_ref, 1), rows_ref[:, :D])[:HEAD].astype(BF16)
    out_ref[...] = dot(lined(own_ref, 0), rows_ref[:, D:])[:HEAD].astype(BF16)


def weights_kernel(
    r_ref, query_ref, out_ref, own_ref, both_ref, rows_ref,
    ret_ref, kept_ref, plus_ref, minus_ref, across_ref,
):
    position = r_ref[0]
    for s in range(PEERS):
        ret_ref[s, : 2 * ROWS] = own_ref[s]
        ret_ref[s, 2 * ROWS :] = both_ref[s]
    inner = jnp.concatenate([lined(ret_ref, 2), lined(ret_ref, 3)], axis=0)
    inner = dot(inner, rows_ref[:, :D])
    for part in range(SETS):
        for step, ref in enumerate((kept_ref, plus_ref, across_ref, minus_ref)):

            @pl.when(((part - position) & 3) == step)
            def _():
                if part == 0:
                    ref[...] = query_ref[...]
                elif part == 3:
                    ref[...] = out_ref[...]
                else:
                    first = (part - 1) * ROWS
                    ref[...] = inner[first : first + HEAD].astype(BF16)


def leave_kernel(slot_ref, seg_ref, ret_ref, packed_ref, mod_ref, cot_ref, win_far, wo_far, out_ref, back_ref, win_ref, wo_ref, sems):
    win_copy = pltpu.make_async_copy(win_far, win_ref, sems.at[0])
    wo_copy = pltpu.make_async_copy(wo_far, wo_ref, sems.at[1])
    wo_copy.start()
    win_copy.start()

    def turned(place):
        return [
            ret_ref[h, place * ROWS : (place + 1) * ROWS].astype(F32)[0:HEAD] for h in range(HEADS)
        ]

    per_token = image_rows(seg_ref[...], mod_ref[...])
    scale = 1.0 + per_token[:, D : 2 * D]
    values = packed_ref[...].astype(F32)
    normed, inverse_spread = normalize(values)
    attended = jnp.concatenate(turned(0), axis=0).T.astype(BF16)
    wo_copy.wait()
    out_ref[...] = (values + per_token[:, 2 * D :] * dot(attended, wo_ref[...])).astype(BF16)
    cot = jnp.concatenate(turned(1) + turned(2) + turned(3), axis=0).T.astype(BF16)
    win_copy.wait()
    scaled = dot(cot, win_ref[...]) * scale
    packed_cot = cot_ref[...].astype(F32) + inverse_spread * (
        scaled
        - jnp.mean(scaled, axis=-1, keepdims=True)
        - normed * jnp.mean(scaled * normed, axis=-1, keepdims=True)
    )
    back_ref[...] = dot(permutation(slot_ref[...]), packed_cot.astype(BF16)).astype(BF16)


def shards(
    owned_patches,
    send_rows,
    receive_slot,
    segment_ids,
    class_label,
    drop_mask,
    class_table,
    modulation_weight,
    attention_in,
    attention_out,
    cotangent,
):
    slot, seg, cot = receive_slot[0], segment_ids, cotangent[0]
    spots = jnp.arange(TOK, dtype=jnp.int32)
    send_hot = send_rows[0, 0][:, None] == spots[None, :]
    outgoing = dot(send_hot.astype(BF16), owned_patches[0]).astype(BF16)
    class_label, outgoing = lax.optimization_barrier((class_label, outgoing))
    incoming = lax.all_to_all(
        outgoing.reshape(32, TOK // 32, D), "seq", split_axis=0, concat_axis=0, tiled=True
    ).reshape(TOK, D)
    chosen = jnp.where(drop_mask[0] == 1, CLASSES, class_label[0])
    condition = jnp.take(class_table, chosen, axis=0)
    activated = jax.nn.silu(condition.astype(F32)).astype(BF16)
    modulation = dot(activated, modulation_weight)
    turned_in = attention_in.T

    packed, rows, pairs, queries = call(
        enter_kernel,
        (
            shape(TOK, D),
            shape(TOK, 2 * D),
            shape(HEADS, 2 * ROWS, TOK),
            shape(HEADS, 2 * ROWS, TOK),
        ),
        n_in=7,
        limit=61,
        far_in=(4, 6),
        far_out=(1, 2, 3),
        scratch=(
            pltpu.VMEM((3 * ATT, D), BF16),
            pltpu.VMEM((ATT, D), BF16),
            pltpu.VMEM((TOK, 2 * D), BF16),
            pltpu.VMEM((HEADS, 2 * ROWS, TOK), BF16),
            pltpu.VMEM((HEADS, 2 * ROWS, TOK), BF16),
            pltpu.SemaphoreType.DMA((5,)),
        ),
        flops=2 * TOK * D * 4 * ATT,
    )(slot, seg, incoming, modulation, turned_in, cot, attention_out)
    all_rows = lax.all_gather(rows, "seq", axis_index_groups=HEAD_GROUPS, tiled=True)

    def trade(array):
        return lax.all_to_all(
            array, "seq", split_axis=0, concat_axis=0, axis_index_groups=HEAD_GROUPS, tiled=True
        )

    pairs = trade(pairs)
    pairs, queries = lax.optimization_barrier((pairs, queries))
    below = lax.ppermute(pairs, "seq", UP)
    above = lax.ppermute(pairs, "seq", DOWN)
    far = lax.ppermute(pairs, "seq", ACROSS)
    queries = trade(queries)

    own, mine, plus, minus, front, rear = attend_call(queries, pairs, below, above, far)

    def add(a, b):
        return (a.astype(F32) + b.astype(F32)).astype(BF16)

    ahead = lax.ppermute(front, "seq", UP)
    behind = lax.ppermute(rear, "seq", DOWN)
    plus = jnp.concatenate([add(plus[:FRONT], ahead), plus[FRONT:]], axis=0)
    minus = jnp.concatenate([minus[:FRONT], add(minus[FRONT:], behind)], axis=0)
    first = lax.ppermute(plus, "seq", UP)
    second = lax.ppermute(minus, "seq", DOWN)
    both = (mine.astype(F32) + first.astype(F32) + second.astype(F32)).astype(BF16)
    position = (lax.axis_index("seq") // PEERS).astype(jnp.int32).reshape(1)
    part = shape(HEAD, D)
    query_part, out_part = call(
        query_weights_kernel,
        (part, part),
        n_in=2,
        limit=16,
        flops=2 * 2 * ROWS * OWN * D,
    )(own, all_rows)
    returning, kept, plus, minus, across = call(
        weights_kernel,
        (shape(PEERS, 4 * ROWS, TOK), part, part, part, part),
        smem=1,
        n_in=6,
        limit=16,
        flops=2 * 2 * ROWS * OWN * D,
    )(position, query_part, out_part, own, both, all_rows)

    piece = kept.astype(F32)
    for block, hop in ((plus, UP), (minus, DOWN), (across, ACROSS)):
        piece = piece + lax.ppermute(block, "seq", hop).astype(F32)
    piece = piece.astype(BF16)
    others = [
        lax.ppermute(piece, "grp", [(i, (i + k) % 4) for i in range(4)]) for k in (1, 3, 2)
    ]
    norm_factor = (4 * 32 * TOK) ** (-0.5)
    summed = piece.astype(F32)
    for other in others:
        summed = summed + other.astype(F32)
    summed = (summed * norm_factor).astype(BF16)
    summed, returning = lax.optimization_barrier((summed, returning))
    gathered = lax.all_gather(summed, "seq", tiled=True)
    gradient_in = gathered[: 3 * ATT].T
    gradient_out = gathered[3 * ATT :]

    returned = trade(returning)
    layer_output, back_order = call(
        leave_kernel,
        (shape(TOK, D), shape(TOK, D)),
        n_in=8,
        limit=61,
        far_in=(6, 7),
        scratch=(
            pltpu.VMEM((3 * ATT, D), BF16),
            pltpu.VMEM((ATT, D), BF16),
            pltpu.SemaphoreType.DMA((2,)),
        ),
        flops=2 * TOK * D * 4 * ATT,
    )(slot, seg, returned, packed, modulation, cot, turned_in, attention_out)
    home = lax.all_to_all(
        back_order.reshape(32, TOK // 32, D), "seq", split_axis=0, concat_axis=0, tiled=True
    ).reshape(TOK, D)
    home_hot = spots[:, None] == send_rows[0, 0][None, :]
    owner_gradient = dot(home_hot.astype(BF16), home).astype(BF16)
    return (layer_output[None], owner_gradient[None], gradient_in, gradient_out)


def solution(mesh):
    return jax.shard_map(
        shards,
        mesh=mesh,
        in_specs=(
            P("grp", "seq", None),
            P("grp", "seq", None),
            P("grp", "seq", None),
            P("grp", "seq"),
            P("grp", None),
            P("grp", None),
            P(),
            P(),
            P(),
            P(),
            P("grp", "seq", None),
        ),
        out_specs=(P("grp", "seq", None), P("grp", "seq", None), P(), P()),
        check_vma=False,
    )
```
